128 devices in a mesh: nodes: 32 (over y, z, core), cores: 4 (over x).
Axes of the slice: x: 4, y: 4, z: 4, core: 2. Of those that a mesh axis runs over, the one named last changes fastest.
Arguments:
- coupling: float32 [98304, 384], P(('nodes', 'cores')), may hold values from -0.4 to 0.4
- onsite: float32 [98304], P(('nodes', 'cores')), may hold values from -3 to 3
- row_slot: int32 [98304], replicated, may hold values from 0 to 98303, as said below
- sub_rows: int32 [192, 1024], replicated, may hold values from 0 to 98303, as said below
- sub_host: int32 [192], replicated, may hold values from 0 to 127, as said below
- branches: int32 [3, 192], replicated, may hold values from 0 to 1
Outputs:
- core_density: float32 [256, 512, 1024], P(('nodes', 'cores'))
- occupation: float32 [3], replicated
The draws below stay inside these ranges and needn't reach their ends.
Inputs may be any that keep to these rules, and one draw needn't show every extreme that they name: `row_slot`: a permutation of the slots; the device holding slot q is q // 768; rows whose numbers are congruent modulo the number of devices are held by the same device. `sub_rows`: each subgraph's rows are 1024 consecutive row numbers modulo 98304; its core rows (positions 256 to 767) of all subgraphs together cover every row once. `sub_host`: every device hosts one or two subgraphs, half of the devices two.
All inputs are finite; a program needn't handle non-finite values.
Results may differ from the reference program's by a relative error of at most 0.0003.
Values sent between devices are 32-bit elements; how exact they have to be, the bound alone decides.
No kernel may reach another device: no remote copies, remote signals or barrier semaphores. Data moves between devices by JAX's collectives and lax.ppermute only.
A program may use at most 128 MiB of HBM per device.

```python
import jax
import jax.numpy as jnp
from jax import lax

CORE = 512
HALO = 256
W = 384
ITERS = 3
M = 1024
NSUB = 192
N_ORB = 98304
ORB_DEV = 768
SLOTS = 256
N_NODES = 32
N_CORES = 4


def draw_row_slot(key, part):
    key = jax.random.fold_in(key, 11)
    first_key, second_key = jax.random.split(key)
    device_count = N_NODES * N_CORES
    owners = jax.random.permutation(first_key, device_count).astype(jnp.int32)
    scores = jax.random.randint(second_key, (device_count, ORB_DEV), 0, 1 << 20)
    local_order = jnp.argsort(scores * ORB_DEV + jnp.arange(ORB_DEV, dtype=jnp.int32)[None, :], axis=1).astype(jnp.int32)
    row_ids = jnp.arange(N_ORB, dtype=jnp.int32)
    holder = owners[row_ids % device_count]
    return (holder * ORB_DEV + local_order[holder, row_ids // device_count]).astype(jnp.int32)


def draw_sub_rows(key, part):
    key = jax.random.fold_in(key, 12)
    order = jax.random.permutation(key, NSUB).astype(jnp.int32)
    starts = order * CORE - HALO
    return jnp.mod(starts[:, None] + jnp.arange(M, dtype=jnp.int32)[None, :], N_ORB).astype(jnp.int32)


def draw_sub_host(key, part):
    key = jax.random.fold_in(key, 13)
    first_key, second_key = jax.random.split(key)
    device_count = N_NODES * N_CORES
    extra = jax.random.permutation(first_key, device_count)[:device_count // 2].astype(jnp.int32)
    hosts = jnp.concatenate([jnp.arange(device_count, dtype=jnp.int32), extra])
    return hosts[jax.random.permutation(second_key, NSUB)].astype(jnp.int32)


def with_ends(drawn, key, least, top_value):
    shape = drawn.shape
    index_at = [jax.random.randint(jax.random.fold_in(key, axis), (), 0, shape[axis]) for axis in range(len(shape))]
    drawn = drawn.at[tuple(index_at)].set(least)
    longest = shape.index(max(shape))
    index_at[longest] = (index_at[longest] + 1) % shape[longest]
    return drawn.at[tuple(index_at)].set(top_value)


def block_levels(rng, extent, cuts, least, high):
    factor_of = 1.0
    for axis_at, parts in cuts:
        heights = jax.random.uniform(jax.random.fold_in(jax.random.fold_in(rng, 6), axis_at), (parts,), jnp.float32, least / len(cuts), high / len(cuts))
        factor_of = factor_of * jnp.repeat(jnp.exp(heights), extent[axis_at] // parts).reshape((-1,) + (1,) * (len(extent) - 1 - axis_at))
    return factor_of


def normal_values(key, dims, width, bound, cuts=(), kind=jnp.bfloat16):
    drawn = width * jax.random.normal(key, dims, jnp.float32)
    if cuts:
        drawn = drawn * block_levels(key, dims, cuts, -0.22, 0.18)
    return jnp.clip(drawn, -bound, bound).astype(kind)


def setup_inputs(seed: int = 0) -> dict:
    streams_of = jax.random.split(jax.random.key(seed), 7)
    coupling = normal_values(streams_of[0], (N_ORB, W), 0.06, 0.4, ((0, 128),), jnp.float32)
    onsite = normal_values(streams_of[1], (N_ORB,), 0.5, 3.0, ((0, 128),), jnp.float32)
    row_slot = draw_row_slot(jax.random.fold_in(streams_of[6], 71), 0)
    sub_rows = draw_sub_rows(jax.random.fold_in(streams_of[6], 71), 0)
    sub_host = draw_sub_host(jax.random.fold_in(streams_of[6], 71), 0)
    branches = with_ends(jax.random.randint(streams_of[5], (ITERS, NSUB), 0, 2), jax.random.fold_in(streams_of[5], 1), 0, 1).astype(jnp.int32)
    return {"coupling": coupling, "onsite": onsite, "row_slot": row_slot, "sub_rows": sub_rows, "sub_host": sub_host, "branches": branches}


decay_length = 256.0
epsilon = 1e-06

def assemble(window_rows, near_rows, site_energy):
    distance = jnp.mod(window_rows[None, :] - window_rows[:, None], N_ORB)
    column = jnp.clip(distance - 1, 0, W - 1)
    picked = jnp.take_along_axis(near_rows, column, axis=1)
    falloff = jnp.exp(-distance.astype(jnp.float32) / decay_length)
    upper_part = jnp.where((distance >= 1) & (distance <= W), picked * falloff, 0.0)
    return upper_part + upper_part.T + jnp.diag(site_energy)

def spectral_edge(hamiltonian, site_energy):
    off_diagonal = hamiltonian - jnp.diag(site_energy)
    radius = 2.0 * jnp.sqrt(lax.optimization_barrier(jnp.sum(off_diagonal * off_diagonal, axis=1)) + epsilon)
    return (jnp.max(site_energy + radius), jnp.min(site_energy - radius))

def reference(coupling, onsite, row_slot, sub_rows, sub_host, branches):

    def fetch(window_rows):
        slot_rows = row_slot[window_rows]
        site_energy = onsite[slot_rows]
        return (assemble(window_rows, coupling[slot_rows], site_energy), site_energy)

    def edges(window_rows):
        hamiltonian, site_energy = fetch(window_rows)
        return spectral_edge(hamiltonian, site_energy)
    highs, lows = lax.map(edges, sub_rows)
    spectrum_top = jnp.max(highs)
    spectrum_bottom = jnp.min(lows)

    def purify(inputs):
        window_rows, sub_branches = inputs
        hamiltonian, site_energy = fetch(window_rows)
        identity = jnp.eye(M, dtype=jnp.float32)
        matrix = (spectrum_top * identity - hamiltonian) / (spectrum_top - spectrum_bottom)
        traces = []
        for iteration in range(ITERS):
            square = jnp.dot(matrix, matrix, precision=lax.Precision.HIGHEST, preferred_element_type=jnp.float32)
            matrix = jnp.where(sub_branches[iteration] == 0, square, 2.0 * matrix - square)
            traces.append(jnp.trace(matrix[HALO:HALO + CORE, HALO:HALO + CORE]))
        return (matrix[HALO:HALO + CORE], jnp.stack(traces))
    densities, traces = lax.map(purify, (sub_rows, branches.T))
    occupation = lax.optimization_barrier(jnp.sum(traces, axis=0)) / N_ORB
    sub_ids = jnp.arange(NSUB, dtype=jnp.int32)
    earlier = (sub_host[:, None] == sub_host[None, :]) & (sub_ids[None, :] < sub_ids[:, None])
    host_slot = (sub_host * 2 + lax.optimization_barrier(jnp.sum(earlier, axis=1))).astype(jnp.int32)
    core_density = jnp.zeros((SLOTS, CORE, M), jnp.float32).at[host_slot].set(densities)
    return (core_density, occupation)
```

```python
import jax
import jax.numpy as jnp
from jax import lax
from jax.experimental import pallas as pl
from jax.experimental.pallas import tpu as pltpu
from jax.sharding import PartitionSpec as P

CORE = 512
HALO = 256
W = 384
ITERS = 3
M = 1024
NSUB = 192
N_ORB = 98304
ORB_DEV = 768
DEVICES = 128
PER_OWNER = 8
UNITS = 21
MESSAGE = 2 * UNITS + 1
FIRST_UNIT = (0, 8, 15)
BLOCK = 256
GRID = M // BLOCK
UPPER = [(i, j) for j in range(GRID) for i in range(j + 1)]
SLOT_LANES = 16
AXES = ("nodes", "cores")
CHUNKS = 8
PACK_VMEM = 58 * 2**20
POWERS_VMEM = 24 * 2**20
FINISH_VMEM = 18 * 2**20

decay_length = 256.0
epsilon = 1e-06

F32 = jnp.float32
BF16 = jnp.bfloat16


def upper_index(i, j):
    return j * (j + 1) // 2 + i


def split3(x):
    a = x.astype(BF16)
    r = x - a.astype(F32)
    b = r.astype(BF16)
    c = (r - b.astype(F32)).astype(BF16)
    return a, b, c


def split2(x):
    a = x.astype(BF16)
    return a, (x - a.astype(F32)).astype(BF16)


def dot(a, b):
    return jnp.dot(a, b, preferred_element_type=F32)


def dot3(ah, al, bh, bl):
    return dot(jnp.concatenate([ah, ah, al], axis=1), jnp.concatenate([bh, bl, bh], axis=0))


def dot_diagonal(ah, bh, bl):
    cross = dot(ah, bl)
    return dot(ah, bh) + (cross + cross.T)


def span(first, last):
    return slice(first * BLOCK, (last + 1) * BLOCK)


def pick_rows(onehot, x):
    y = dot(onehot, jnp.concatenate(split2(x), axis=1))
    return y[:, 0:128] + y[:, 128:256]


def pick_rows_exact(onehot, x):
    a, b, c = split3(x)
    return dot(onehot, a) + dot(onehot, b) + dot(onehot, c)


def pack_kernel(dev_ref, host_ref, subs_hbm, rows_hbm, coup_hbm, ons_ref, out_ref, meta_ref,
                start_ref, rows_ref, coup_ref, held_ref, send_ref, count_ref, table_ref, sems, out_sems):
    load_subs = pltpu.make_async_copy(subs_hbm.at[:, pl.ds(0, 128)], start_ref, sems.at[0])
    load_rows = pltpu.make_async_copy(rows_hbm, rows_ref, sems.at[1])
    load_coup = pltpu.make_async_copy(coup_hbm, coup_ref, sems.at[2])
    load_rows.start()
    load_subs.start()
    load_coup.start()
    dev = dev_ref[0]

    @pl.loop(0, DEVICES, unroll=8)
    def _(h):
        count_ref[h] = 0
        table_ref[2 * h + 1] = 0

    @pl.loop(0, NSUB, unroll=8)
    def _(s):
        h = host_ref[s]
        k = count_ref[h]
        count_ref[h] = k + 1
        table_ref[2 * h + k] = s

    load_rows.wait()
    rel = rows_ref[...] - dev * ORB_DEV
    mine = (rel >= 0) & (rel < ORB_DEV)
    relf = jnp.where(mine, rel.astype(F32), 0.0)
    local = jnp.sum(relf, axis=1, keepdims=True)
    lane = lax.broadcasted_iota(jnp.int32, (8, DEVICES), 1)
    residue = (jnp.sum(jnp.where(mine[0:8], lane.astype(F32), 0.0)) * 0.125).astype(jnp.int32)
    slot_lane = lax.broadcasted_iota(jnp.int32, (ORB_DEV, ORB_DEV), 1)
    pick = slot_lane == local.astype(jnp.int32)
    onehot = jnp.where(pick, 1.0, 0.0).astype(BF16)
    onsite = jnp.concatenate([ons_ref[q:q + 1, :] for q in range(ORB_DEV // 128)], axis=1)
    energy = jnp.sum(jnp.where(pick, onsite, 0.0), axis=1, keepdims=True)
    distance = lax.broadcasted_iota(jnp.int32, (1, W), 1) + 1
    falloff = jnp.exp(-distance.astype(F32) / decay_length)
    load_coup.wait()
    for c in range(3):
        cols = slice(c * 128, (c + 1) * 128)
        parts = coup_ref[:, cols]
        for r in range(0, ORB_DEV, BLOCK):
            part = pick_rows(onehot[r:r + BLOCK], parts) * falloff[:, cols]
            held_ref[c, r:r + BLOCK, :] = part
            if r == 0:
                held_ref[c, ORB_DEV:ORB_DEV + 8, :] = part[0:8]
    lanes = lax.broadcasted_iota(jnp.int32, (ORB_DEV, 128), 1)
    diag = jnp.broadcast_to(energy, (ORB_DEV, 128))
    for t in (1, 2, 4):
        diag = jnp.where((lanes & t) == 0, diag, pltpu.roll(diag, ORB_DEV - t, 0))
    held_ref[3, 0:ORB_DEV, :] = diag
    held_ref[3, ORB_DEV:ORB_DEV + 8, :] = diag[0:8]

    load_subs.wait()
    used = jnp.where(count_ref[dev] > 1, 1, 0)
    first_sub = table_ref[2 * dev]
    second_sub = jnp.where(used == 1, table_ref[2 * dev + 1], first_sub)
    meta_ref[0] = start_ref[first_sub, 0]
    meta_ref[1] = start_ref[second_sub, 0]
    meta_ref[2] = used
    meta_ref[3] = first_sub
    meta_ref[4] = second_sub
    meta_ref[5] = dev

    lane1 = lax.broadcasted_iota(jnp.int32, (1, 128), 1)
    chunk = DEVICES // CHUNKS
    copies = []
    for q in range(CHUNKS):

        @pl.loop(q * chunk, (q + 1) * chunk, unroll=4)
        def _(h):
            energies = []
            for k in range(2):
                first = lax.shift_right_arithmetic(start_ref[table_ref[2 * h + k], 0] - residue + 127, 7)
                first = jnp.where(first >= ORB_DEV, first - ORB_DEV, first)
                for c in range(3):
                    at = h * MESSAGE + k * UNITS + FIRST_UNIT[c]
                    send_ref[pl.ds(at, 8), :] = held_ref[c, pl.ds(first, 8), :]
                energies.append(held_ref[3, pl.ds(first, 1), :])
            send_ref[pl.ds(h * MESSAGE + 2 * UNITS, 1), :] = jnp.where(lane1 < 8, energies[0], energies[1])

        part = pl.ds(q * chunk * MESSAGE, chunk * MESSAGE)
        copies.append(pltpu.make_async_copy(send_ref.at[part], out_ref.at[part], out_sems.at[q]))
        copies[-1].start()
    for copy in copies:
        copy.wait()


def pack(dev, sub_host, sub_rows, rows2d, coupling, onsite2d):
    smem = pl.BlockSpec(memory_space=pltpu.SMEM)
    vmem = pl.BlockSpec(memory_space=pltpu.VMEM)
    hbm = pl.BlockSpec(memory_space=pl.ANY)
    return pl.pallas_call(
        pack_kernel,
        out_shape=(
            jax.ShapeDtypeStruct((DEVICES * MESSAGE, 128), F32),
            jax.ShapeDtypeStruct((16,), jnp.int32),
        ),
        in_specs=[smem, smem, hbm, hbm, hbm, vmem],
        out_specs=(hbm, smem),
        scratch_shapes=[
            pltpu.SMEM((NSUB, 128), jnp.int32),
            pltpu.VMEM((ORB_DEV, DEVICES), jnp.int32),
            pltpu.VMEM((ORB_DEV, W), F32),
            pltpu.VMEM((4, ORB_DEV + 16, 128), F32),
            pltpu.VMEM((DEVICES * MESSAGE + 8, 128), F32),
            pltpu.SMEM((DEVICES,), jnp.int32),
            pltpu.SMEM((2 * DEVICES,), jnp.int32),
            pltpu.SemaphoreType.DMA((3,)),
            pltpu.SemaphoreType.DMA((CHUNKS,)),
        ],
        compiler_params=pltpu.CompilerParams(vmem_limit_bytes=PACK_VMEM),
        name="pack",
    )(dev, sub_host, sub_rows, rows2d, coupling, onsite2d)


def store_both(hi_ref, lo_ref, i, j, size, block):
    hi, lo = split2(block)
    hi_ref[i * size:(i + 1) * size, j * size:(j + 1) * size] = hi
    lo_ref[i * size:(i + 1) * size, j * size:(j + 1) * size] = lo


def build_powers(out, slot, meta_ref, branch_ref, rows_ref, got_ref, pw_ref, hh, hl, gh, gl):
    start = meta_ref[slot]
    owner = ((rows_ref[0:8].astype(F32) + 0.5) * (1.0 / ORB_DEV)).astype(jnp.int32)
    shift = lax.rem(DEVICES - lax.rem(start, DEVICES), DEVICES)
    owner = pltpu.roll(owner, shift, 1)[0:1]
    source = lax.broadcasted_iota(jnp.int32, (DEVICES, DEVICES), 0)
    onehot = jnp.where(source == owner, 1.0, 0.0).T.astype(BF16)

    def received(unit):
        return got_ref[pl.ds(unit, DEVICES, stride=MESSAGE), :]

    energies = pick_rows_exact(onehot, received(2 * UNITS)).T[8 * slot:8 * slot + 8]
    center = 0.5 * (jnp.max(energies) + jnp.min(energies))
    row = lax.broadcasted_iota(jnp.int32, (128, 128), 0)
    col = lax.broadcasted_iota(jnp.int32, (128, 128), 1)
    zero = jnp.zeros((128, 128), F32)
    for bi, bj in ((0, 5), (2, 7)):
        pw_ref[0, upper_index(bi // 2, bj // 2), 0:128, 128:256] = zero
    square_sums = [jnp.zeros((1, 128), F32) for _ in range(8)]

    def put(bi, bj, block):
        i, j = bi // 2, bj // 2
        if i <= j:
            ri, rj = (bi % 2) * 128, (bj % 2) * 128
            pw_ref[0, upper_index(i, j), ri:ri + 128, rj:rj + 128] = block
        store_both(hh, hl, bi, bj, 128, block)

    for t in range(8):
        count = min(3, 8 - t)
        near = [pick_rows(onehot, received(slot * UNITS + FIRST_UNIT[c] + t)) for c in range(count)]
        skewed = pltpu.roll(jnp.concatenate(near + [zero], axis=1), 1, 1, stride=1, stride_axis=0)
        for k in range(count + 1):
            if t + k > 7:
                continue
            upper = skewed[:, k * 128:(k + 1) * 128]
            lower = upper.T
            if k == 0:
                both = upper + lower
                square_sums[t] += jnp.sum(both * both, axis=0, keepdims=True)
                put(t, t, both + jnp.where(row == col, energies[t:t + 1] - center, 0.0))
            else:
                square_sums[t + k] += jnp.sum(upper * upper, axis=0, keepdims=True)
                square_sums[t] += jnp.sum(lower * lower, axis=0, keepdims=True)
                put(t, t + k, upper)
                put(t + k, t, lower)
        if t < 4:
            put(t, t + 4, zero)
            put(t + 4, t, zero)
        yield
    radius = 2.0 * jnp.sqrt(jnp.concatenate(square_sums, axis=0) + epsilon)
    top = jnp.max(energies + radius)
    low = jnp.max(radius - energies)

    weights = {(0, 1): 1.0, (0, 2): 1.0, (1, 1): 1.0, (1, 2): 2.0, (1, 3): 1.0, (2, 2): 1.0, (2, 3): 1.0}
    sums = [jnp.zeros((1, BLOCK), F32) for _ in range(9)]

    def add_moment(k, i, j, a, b):
        if (i, j) in weights:
            part = jnp.sum(a * b, axis=0, keepdims=True)
            sums[k] = sums[k] + (part if weights[i, j] == 1.0 else weights[i, j] * part)

    eye = lax.broadcasted_iota(jnp.int32, (BLOCK, BLOCK), 0) == lax.broadcasted_iota(jnp.int32, (BLOCK, BLOCK), 1)

    def keep(p, i, j, block, moments):
        at = upper_index(i, j)
        pw_ref[p, at] = block
        if i == j and (i, j) in weights:
            sums[p + 1] = sums[p + 1] + jnp.sum(jnp.where(eye, block, 0.0), axis=0, keepdims=True)
        for q in moments:
            add_moment(p + q + 2, i, j, block, block if p == q else pw_ref[q, at])

    def square():
        for j in range(GRID):
            for i in range(j + 1):
                mid = slice(max(0, j * BLOCK - W), min(M, (i + 1) * BLOCK + W))
                rows, cols = span(i, i), span(j, j)
                if i == j:
                    block = dot_diagonal(hh[rows, mid], hh[mid, cols], hl[mid, cols])
                else:
                    block = dot3(hh[rows, mid], hl[rows, mid], hh[mid, cols], hl[mid, cols])
                keep(1, i, j, block, ())
                store_both(gh, gl, i, j, BLOCK, block)
                if i != j:
                    store_both(gh, gl, j, i, BLOCK, block.T)
            yield

    def product(p, bh, bl, banded, moments):
        for j in range(GRID):
            mid, cols = slice(0, M), span(j, j)
            if banded:
                mid = slice(max(0, j * BLOCK - W), min(M, (j + 1) * BLOCK + W))
            for i in range(j + 1):
                rows = span(i, i)
                if banded and i == 0:
                    near = slice(0, BLOCK + W)
                    block = dot3(bh[rows, near], bl[rows, near], gh[near, cols], gl[near, cols])
                elif i == j and not banded:
                    block = dot_diagonal(gh[rows, mid], bh[mid, cols], bl[mid, cols])
                else:
                    block = dot3(gh[rows, mid], gl[rows, mid], bh[mid, cols], bl[mid, cols])
                keep(p, i, j, block, moments)
            yield

    yield from square()
    yield from product(2, hh, hl, True, (1, 2))
    yield from product(3, gh, gl, False, (2, 3))
    values = [jnp.asarray(float(CORE), F32), jnp.sum(energies[2:6] - center)]
    values += [jnp.sum(s) for s in sums[2:]]
    values += [center] + [branch_ref[t, meta_ref[3 + slot]].astype(F32) for t in range(ITERS)] + [top, low]
    lane = lax.broadcasted_iota(jnp.int32, (8, 128), 1)
    stats = jnp.zeros((8, 128), F32)
    for k, value in enumerate(values):
        stats = jnp.where(lane == slot * SLOT_LANES + k, value, stats)
    out.append(stats)


def powers_kernel(meta_ref, branch_ref, rows_ref, got_ref, pw0, pw1, send_ref, *parts):
    lane = lax.broadcasted_iota(jnp.int32, (8, 128), 1)
    empty = (lane == SLOT_LANES + 13) | (lane == SLOT_LANES + 14)
    first, second = [], []
    steps = [
        build_powers(out, k, meta_ref, branch_ref, rows_ref, got_ref, (pw0, pw1)[k], *parts[4 * k:4 * k + 4])
        for k, out in enumerate((first, second))
    ]
    for _ in range(8):
        next(steps[0])
    for _ in range(8):
        next(steps[0])
        next(steps[1])
    for step in steps:
        for _ in step:
            pass
    first, second = first[0], second[0]
    second = jnp.where(meta_ref[2] == 1, second, jnp.where(empty, -1e30, 0.0))
    send_ref[...] = jnp.broadcast_to((first + second)[0:1], (DEVICES, 128))


def powers(meta, branches, rows2d, got):
    smem = pl.BlockSpec(memory_space=pltpu.SMEM)
    vmem = pl.BlockSpec(memory_space=pltpu.VMEM)
    return pl.pallas_call(
        powers_kernel,
        out_shape=(
            jax.ShapeDtypeStruct((4, len(UPPER), BLOCK, BLOCK), F32),
            jax.ShapeDtypeStruct((4, len(UPPER), BLOCK, BLOCK), F32),
            jax.ShapeDtypeStruct((DEVICES, 128), F32),
        ),
        in_specs=[smem, smem, vmem, vmem],
        out_specs=(vmem, vmem, vmem),
        scratch_shapes=[pltpu.VMEM((M, M), BF16)] * 8,
        compiler_params=pltpu.CompilerParams(vmem_limit_bytes=POWERS_VMEM),
        name="powers",
    )(meta, branches, rows2d, got)


def purify(poly, branch):
    squared = [None] * (2 * len(poly) - 1)
    for a, pa in enumerate(poly):
        for b in range(a, len(poly)):
            term = pa * poly[b] if a == b else 2.0 * pa * poly[b]
            squared[a + b] = term if squared[a + b] is None else squared[a + b] + term
    other = [2.0 * poly[k] - value if k < len(poly) else -value for k, value in enumerate(squared)]
    return [jnp.where(branch == 0, value, out) for value, out in zip(squared, other)]


def finish_kernel(meta_ref, branch_ref, recv_ref, pw0, pw1, core_ref, occ_ref, xh0, xl0, xh1, xl1, out_ref, out_sems):
    used = meta_ref[2]
    dev = meta_ref[5]
    lane = lax.broadcasted_iota(jnp.int32, (1, 128), 1)
    most = jnp.max(recv_ref[...], axis=0, keepdims=True)
    top = jnp.max(jnp.where((lane == 13) | (lane == SLOT_LANES + 13), most, -1e30))
    low = jnp.max(jnp.where((lane == 14) | (lane == SLOT_LANES + 14), most, -1e30))
    own = recv_ref[pl.ds(dev, 1), :]
    scale = 1.0 / jnp.broadcast_to(top + low, (1, BLOCK))
    coefs = []
    for slot in range(2):
        center = jnp.sum(jnp.where(lane == SLOT_LANES * slot + 9, own, 0.0))
        poly = [(top - center) * scale, -scale]
        for t in range(2):
            poly = purify(poly, branch_ref[t, meta_ref[3 + slot]])
        coefs.append(poly)

    def occupation():
        table = recv_ref[...].T
        totals = [jnp.zeros((1, 128), F32) for _ in range(ITERS)]
        for slot in range(2):
            base = SLOT_LANES * slot
            poly = [(top - table[base + 9:base + 10]) * scale[:, 0:128], -scale[:, 0:128]]
            for t in range(ITERS):
                poly = purify(poly, table[base + 10 + t:base + 11 + t])
                for k, value in enumerate(poly):
                    totals[t] = totals[t] + value * table[base + k:base + k + 1]
        for t in range(ITERS):
            occ_ref[t] = jnp.sum(totals[t]) * (1.0 / N_ORB)

    row = lax.broadcasted_iota(jnp.int32, (BLOCK, BLOCK), 0)
    col = lax.broadcasted_iota(jnp.int32, (BLOCK, BLOCK), 1)

    def store(slot, j):
        cols = pl.ds(j * BLOCK, BLOCK)
        return pltpu.make_async_copy(
            out_ref.at[slot, :, cols], core_ref.at[slot, :, cols], out_sems.at[slot, j]
        )

    def form(slot):
        c = coefs[slot]
        pw_ref = (pw0, pw1)[slot]
        xh, xl = ((xh0, xl0), (xh1, xl1))[slot]
        constant = jnp.where(row == col, c[0], 0.0)
        for i, j in UPPER:
            at = upper_index(i, j)
            block = c[2] * pw_ref[1, at]
            for p in range(0 if j - i < GRID - 1 else 2, 4):
                if p != 1:
                    block = block + c[p + 1] * pw_ref[p, at]
            if i == j:
                block = block + constant
            hi, lo = split2(block)
            xh[span(i, i), span(j, j)] = hi
            xl[span(i, i), span(j, j)] = lo
            if i != j:
                xh[span(j, j), span(i, i)] = hi.T
                xl[span(j, j), span(i, i)] = lo.T
            yield

    def last_square(slot):
        xh, xl = ((xh0, xl0), (xh1, xl1))[slot]
        branch = branch_ref[ITERS - 1, meta_ref[3 + slot]]

        def put(i, j, acc):
            rows, cols = span(i, i), span(j, j)
            x = xh[rows, cols].astype(F32) + xl[rows, cols].astype(F32)
            value = jnp.where(branch == 0, acc, 2.0 * x - acc)
            out_ref[slot, span(i - 1, i - 1), cols] = value if slot == 0 else jnp.where(used == 1, value, 0.0)

        for j in (0, 2, 1, 3):
            cols = span(j, j)
            for i in (1, 2):
                rows = span(i, i)
                if (i, j) == (2, 1):
                    continue
                if i == j:
                    put(i, j, dot_diagonal(xh[rows, :], xh[:, cols], xl[:, cols]))
                    continue
                acc = dot3(xh[rows, :], xl[rows, :], xh[:, cols], xl[:, cols])
                put(i, j, acc)
                if (i, j) == (1, 2):
                    put(2, 1, acc.T)
            store(slot, j).start()
            yield

    for _ in form(0):
        pass
    occupation()
    forming = form(1)
    for _ in last_square(0):
        for _ in range(3):
            next(forming, None)
    for _ in last_square(1):
        pass
    for slot in range(2):
        for j in range(GRID):
            store(slot, j).wait()


def finish(meta, branches, recv, pw0, pw1):
    smem = pl.BlockSpec(memory_space=pltpu.SMEM)
    vmem = pl.BlockSpec(memory_space=pltpu.VMEM)
    hbm = pl.BlockSpec(memory_space=pl.ANY)
    return pl.pallas_call(
        finish_kernel,
        out_shape=(
            jax.ShapeDtypeStruct((2, CORE, M), F32),
            jax.ShapeDtypeStruct((ITERS,), F32),
        ),
        in_specs=[smem, smem, vmem, vmem, vmem],
        out_specs=(hbm, smem),
        scratch_shapes=[
            pltpu.VMEM((M, M), BF16),
            pltpu.VMEM((M, M), BF16),
            pltpu.VMEM((M, M), BF16),
            pltpu.VMEM((M, M), BF16),
            pltpu.VMEM((2, CORE, M), F32),
            pltpu.SemaphoreType.DMA((2, GRID)),
        ],
        compiler_params=pltpu.CompilerParams(vmem_limit_bytes=FINISH_VMEM),
        name="finish",
    )(meta, branches, recv, pw0, pw1)


def exchange(x):
    rows, lanes = x.shape
    blocks = x.reshape(DEVICES, 1, rows // DEVICES * lanes)
    return lax.all_to_all(blocks, AXES, split_axis=0, concat_axis=0, tiled=True).reshape(rows, lanes)


def on_device(coupling, onsite, row_slot, sub_rows, sub_host, branches):
    dev = lax.axis_index(AXES).astype(jnp.int32).reshape(1)
    rows2d = row_slot.reshape(ORB_DEV, DEVICES)
    send, meta = pack(dev, sub_host, sub_rows, rows2d, coupling, onsite.reshape(ORB_DEV // 128, 128))
    pw0, pw1, stats = powers(meta, branches, rows2d, exchange(send))
    return finish(meta, branches, exchange(stats), pw0, pw1)


def solution(mesh):
    return jax.shard_map(
        on_device,
        mesh=mesh,
        in_specs=(P(AXES, None), P(AXES), P(), P(), P(), P()),
        out_specs=(P(AXES, None, None), P()),
        check_vma=False,
    )
```
